32 devices in a mesh: dp: 2 (over y), ep: 16 (over z, x, core).
Axes of the slice: x: 2, y: 2, z: 4, core: 2. Of those that a mesh axis runs over, the one named last changes fastest.
Arguments:
- expert_ids: int32 [2, 256, 8], P('dp', 'ep'), may hold values from 0 to 15, all different within a row; in each aligned block of 16 rows (0 to 15, 16 to 31, ..., all dimensions but the last counted through in order) at most 16 rows name the same one
- route_weights: float32 [2, 256, 8], P('dp', 'ep'), may hold values from 0.03 to 0.4
- saved_rows: bfloat16 [2, 16, 256, 2048], P('dp', 'ep'), may hold values from -6 to 6
- saved_gate_up: bfloat16 [2, 16, 256, 1536], P('dp', 'ep'), may hold values from -6 to 6
- hidden_grad: bfloat16 [2, 16, 256, 768], P('dp', 'ep'), may hold values from -6 to 6
- gate_up_weight: bfloat16 [16, 2048, 1536], P('ep'), may hold values from -0.125 to 0.125
Outputs:
- input_grad: bfloat16 [2, 256, 2048], P('dp', 'ep')
- weight_grad: float32 [2048, 16, 1536], P('dp', 'ep')
The draws below stay inside these ranges and needn't reach their ends.
Inputs may be any that keep to these rules, and one draw needn't show every extreme that they name: `expert_ids`: each token names 8 different experts; among the tokens of one device no expert is named more than 16 times, a bound that some block reaches.
All inputs are finite; a program needn't handle non-finite values.
Results may differ from the reference program's by a relative error of at most 0.017.
Values may be sent and summed in bfloat16 or wider, within the bound.
A program may use at most 64 MiB of HBM per device.

```python
import math
import jax
import jax.numpy as jnp
import numpy as np
from jax import lax

D = 2048
FF = 768
TOP = 8
TOK_DEV = 16
EXPERTS = 16
CAP = 16
SLOTS = 256
TOKENS = 256
N_DP = 2
N_EP = 16


def with_spikes(values, rng, source, target, parts, factor):
    owner, partner = [(jnp.arange(values.shape[position]) // (values.shape[position] // parts)).reshape([-1 if axis == position else 1 for axis in range(values.ndim)]) for position in (source, target)]
    chosen = jax.random.permutation(rng, parts)[partner]
    strong = (owner == chosen) | (owner == (partner + parts // 2) % parts)
    return jnp.where(strong, factor * values, values)


def block_levels(stream_key, dims, pieces, low, top_value):
    def one(position, shards_of):
        draws = jax.random.uniform(jax.random.fold_in(jax.random.fold_in(stream_key, 6), position), (shards_of,), jnp.float32, low / len(pieces), top_value / len(pieces))
        return jnp.repeat(jnp.exp(draws), dims[position] // shards_of).reshape((-1,) + (1,) * (len(dims) - position - 1))

    level = one(*pieces[0])
    for cut in pieces[1:]:
        level = level * one(*cut)
    return level


def routed_block(own_key, own, number, rows, number_of, top, most, skew):
    ranking = jax.random.permutation(own_key, number_of)
    packed, common = shares(number_of, rows * top, most, skew, True), shares(number_of, rows * top, most, skew, False)
    places = jnp.arange(number_of)

    def named(lengths, rotation):
        used = int((lengths > 0).sum())
        fixed = max(1, used // 4)
        passed = fixed + (places - fixed + rotation * (used - fixed)) % max(1, number_of - fixed)
        return jnp.zeros((number_of,), jnp.int32).at[ranking[jnp.where(places < fixed, places, passed)]].set(jnp.asarray(lengths, jnp.int32))

    lengths = jnp.where(number % 4 == 0, named(packed, number // 4), named(common, number - number // 4 - 1))
    mixed = jax.random.permutation(jax.random.fold_in(own, 3), number_of)
    source_of, receiver = mixed[0:number_of // 2 * 2:2], mixed[1:number_of // 2 * 2:2]
    margin = jnp.minimum(lengths[source_of] - 1, most - lengths[receiver]) // 2
    margin = jnp.where((source_of == ranking[0]) | (receiver == ranking[0]) | (lengths[receiver] == 0), 0, jnp.maximum(margin, 0))
    passed = jax.random.randint(jax.random.fold_in(own, 4), (number_of // 2,), 0, 1 << 20) % (margin + 1)
    lengths = lengths.at[source_of].add(-passed).at[receiver].add(passed)
    members = jnp.searchsorted(jnp.cumsum(lengths), jnp.arange(rows * top), side="right").astype(jnp.int32)
    grid = members.reshape(top, rows).T
    grid = grid[jax.random.permutation(jax.random.fold_in(own, 1), rows)]
    rotation = jax.random.randint(jax.random.fold_in(own, 2), (rows, 1), 0, top)
    return jnp.take_along_axis(grid, (jnp.arange(top)[None, :] + rotation) % top, axis=1)


def shares(number_of, total, most, slope, full):
    portions = [(1 << 20) // math.isqrt(rank ** slope) + 1 for rank in range(1, number_of + 1)]
    largest = most if full else min(most, max(-(-total // number_of), total * portions[0] // sum(portions)))
    least = 1 if total - largest >= number_of - 1 else 0
    given, spare = [largest] + [least] * (number_of - 1), total - largest - least * (number_of - 1)
    while spare > 0:
        movable = [i for i in range(1, number_of) if given[i] < largest] or [i for i in range(1, number_of) if given[i] < most]
        mass, remaining = sum([portions[i] for i in movable]), spare
        for i in movable:
            extra = min(most - given[i], max(1, remaining * portions[i] // mass), spare)
            given[i] = given[i] + extra
            spare = spare - extra
    return np.array(given)


def normal_values(rng, dims, width, limit, cuts=(), kind=jnp.bfloat16):
    gain = block_levels(rng, dims, cuts, -0.22, 0.18) if cuts else 1.0
    array = jax.random.normal(rng, dims, jnp.float32) * width * gain
    return jnp.minimum(jnp.maximum(array, -limit), limit).astype(kind)


def heavy_noise(own_key, extent, deviation, bound, split, heavy, kind=jnp.bfloat16):
    drawn = deviation * jax.random.normal(own_key, extent, jnp.float32)
    if split:
        drawn = drawn * block_levels(own_key, extent, split, -0.22, 0.18)
    return jnp.clip(with_spikes(drawn, jax.random.fold_in(own_key, 3), *heavy), -bound, bound).astype(kind)


def setup_inputs(seed: int = 0) -> dict:
    streams_of = jax.random.split(jax.random.key(seed), 7)
    expert_ids_keys = jax.random.split(jax.random.fold_in(streams_of[0], 1), N_DP * TOKENS // TOK_DEV)
    expert_ids_turns = jax.random.permutation(jax.random.fold_in(streams_of[0], 3), N_DP * TOKENS // TOK_DEV)
    expert_ids = jax.vmap(lambda own, number: routed_block(jax.random.fold_in(streams_of[0], 2), own, number, TOK_DEV, EXPERTS, TOP, CAP, 2))(expert_ids_keys, expert_ids_turns).reshape((N_DP, TOKENS, TOP))
    route_weights = jnp.clip(jnp.exp(math.log(0.4) - 2.5902672 * jax.random.uniform(streams_of[1], (N_DP, TOKENS, TOP), jnp.float32) ** block_levels(streams_of[1], (N_DP, TOKENS, TOP), ((0, 2), (1, 16)), -0.2, 0.2)), 0.03, 0.4)
    saved_rows = heavy_noise(streams_of[2], (N_DP, EXPERTS, SLOTS, D), 1.0, 6.0, ((0, 2), (1, 16)), (0, 3, 2, 2.0))
    saved_gate_up = normal_values(streams_of[3], (N_DP, EXPERTS, SLOTS, 2 * FF), 1.5, 6.0, ((0, 2), (1, 16)))
    hidden_grad = normal_values(streams_of[4], (N_DP, EXPERTS, SLOTS, FF), 1.0, 6.0, ((0, 2), (1, 16)))
    gate_up_weight = normal_values(streams_of[5], (EXPERTS, D, 2 * FF), D ** -0.5, 0.125, ((0, 16),))
    return {"expert_ids": expert_ids, "route_weights": route_weights, "saved_rows": saved_rows, "saved_gate_up": saved_gate_up, "hidden_grad": hidden_grad, "gate_up_weight": gate_up_weight}


def route_tables(expert_ids):
    blocks = expert_ids.reshape(N_DP * N_EP, TOK_DEV * TOP)
    onehot = (blocks[:, :, None] == jnp.arange(EXPERTS, dtype=jnp.int32)[None, None, :]).astype(jnp.int32)
    before = (jnp.cumsum(onehot, axis=1) - onehot).astype(jnp.int32)
    rank_in_block = jnp.sum(before * onehot, axis=2).astype(jnp.int32).reshape(N_DP, TOKENS, TOP)
    counts = jnp.sum(onehot, axis=1).astype(jnp.int32).reshape(N_DP, N_EP, EXPERTS)
    return rank_in_block, counts


def reference(expert_ids, route_weights, saved_rows, saved_gate_up, hidden_grad, gate_up_weight):
    rank_in_block, counts = route_tables(expert_ids)
    per_expert = jnp.transpose(counts, (0, 2, 1))
    live_mask = (jnp.arange(CAP, dtype=jnp.int32)[None, None, None, :] < per_expert[..., None]).reshape(N_DP, EXPERTS, SLOTS)
    gate_pre = saved_gate_up[..., :FF].astype(jnp.float32)
    up_pre = saved_gate_up[..., FF:].astype(jnp.float32)
    grad_hidden = hidden_grad.astype(jnp.float32)
    sigma_gate = jax.nn.sigmoid(gate_pre)
    grad_gate = grad_hidden * up_pre * sigma_gate * (1.0 + gate_pre * (1.0 - sigma_gate))
    grad_up = grad_hidden * gate_pre * sigma_gate
    slot_grads = (jnp.concatenate([grad_gate, grad_up], axis=-1) * live_mask[..., None].astype(jnp.float32)).astype(jnp.bfloat16)

    def expert_work(index):
        rows = lax.dynamic_index_in_dim(saved_rows, index, 1, keepdims=False).astype(jnp.float32)
        grads = lax.dynamic_index_in_dim(slot_grads, index, 1, keepdims=False).astype(jnp.float32)
        weight = lax.dynamic_index_in_dim(gate_up_weight, index, 0, keepdims=False).astype(jnp.float32)
        row_grads = jnp.einsum('rsf,df->rsd', grads, weight).astype(jnp.bfloat16)
        partial_value = jnp.einsum('rsd,rsf->rdf', rows, grads)
        rounded = lax.optimization_barrier(partial_value.astype(jnp.bfloat16))
        summed = jnp.sum(rounded.astype(jnp.float32), axis=0) / N_DP
        return row_grads, summed

    row_grads, weight_sums = lax.map(expert_work, jnp.arange(EXPERTS, dtype=jnp.int32))
    replica_index = jnp.arange(N_DP, dtype=jnp.int32)[:, None, None]
    slot_index = ((jnp.arange(TOKENS, dtype=jnp.int32) // TOK_DEV)[None, :, None] * CAP + rank_in_block).astype(jnp.int32)
    picked = row_grads[expert_ids, replica_index, slot_index]
    combined = jnp.sum(route_weights[..., None] * picked.astype(jnp.float32), axis=2)
    input_grad = combined.astype(jnp.bfloat16)
    weight_grad = jnp.transpose(weight_sums, (1, 0, 2))
    return input_grad, weight_grad
```

```python
import functools

import jax
import jax.numpy as jnp
from jax import lax
from jax.experimental import pallas as pl
from jax.experimental.pallas import tpu as pltpu
from jax.sharding import PartitionSpec as P

F32 = jnp.float32
BF16 = jnp.bfloat16
LANES = 128
PIECES = 2
VMEM_LIMIT = 56 * 2**20


def reversed_bits(value, bits):
    out = value * 0
    for b in range(bits):
        out = out * 2 + (value // 2**b) % 2
    return out


def exchange_kernel(
    n_dp, n_ep, stages, ids_ref, route_ref, rows_hbm, gate_up_hbm, hidden_hbm, weight_hbm,
    rows_all, grads_all, token_out,
    route_send, route_recv, route_col, gate_up, hidden, weight, grads, mixed, total,
    load_sem, own_sem, route_ssem, route_rsem, rows_ssem, rows_rsem, grads_ssem, grads_rsem,
    half_ssem, half_rsem, *halves,
):
    sends, recvs = halves[:stages], halves[stages:]
    my_dp = lax.axis_index("dp")
    my_ep = lax.axis_index("ep")
    tokens = ids_ref.shape[1]
    slots, width2 = grads.shape
    width = width2 // 2
    model = weight.shape[0]
    share = model // n_dp
    cap = slots // n_ep
    all_tokens = n_ep * tokens
    piece = model // PIECES

    loads = [
        pltpu.make_async_copy(gate_up_hbm.at[0, 0], gate_up, load_sem.at[0]),
        pltpu.make_async_copy(hidden_hbm.at[0, 0], hidden, load_sem.at[1]),
        pltpu.make_async_copy(weight_hbm.at[0], weight, load_sem.at[2]),
    ]
    for load in loads:
        load.start()

    barrier = pltpu.get_barrier_semaphore()
    for k in range(1, n_ep):
        pl.semaphore_signal(barrier, inc=1, device_id={"ep": lax.rem(my_ep + k, n_ep)}, device_id_type=pl.DeviceIdType.MESH)
    for k in range(1, n_dp):
        pl.semaphore_signal(barrier, inc=1, device_id={"dp": lax.rem(my_dp + k, n_dp)}, device_id_type=pl.DeviceIdType.MESH)

    route_send[...] = jnp.zeros_like(route_send)
    ids = ids_ref[...]
    route = route_ref[...]
    for x in range(n_ep):
        route_send[x, :, 0:tokens] = jnp.sum(jnp.where(ids == x, route, 0.0), axis=0, keepdims=True)
    pl.semaphore_wait(barrier, n_ep - 1 + n_dp - 1)

    my_place = reversed_bits(my_ep, stages)
    route_copies = []
    for k in range(1, n_ep):
        to = lax.rem(my_ep + k, n_ep)
        route_copies.append(pltpu.make_async_remote_copy(
            src_ref=route_send.at[to], dst_ref=route_recv.at[my_place],
            send_sem=route_ssem.at[k], recv_sem=route_rsem.at[k],
            device_id={"ep": to}, device_id_type=pl.DeviceIdType.MESH))
    for copy in route_copies:
        copy.start()
    rows_copies = []
    for k in range(1, n_dp):
        to = lax.rem(my_dp + k, n_dp)
        rows_copies.append(pltpu.make_async_remote_copy(
            src_ref=rows_hbm.at[0, 0, :, pl.ds(pl.multiple_of(to * share, LANES), share)],
            dst_ref=rows_all.at[my_dp],
            send_sem=rows_ssem.at[k], recv_sem=rows_rsem.at[k],
            device_id={"dp": to}, device_id_type=pl.DeviceIdType.MESH))
    for copy in rows_copies:
        copy.start()
    own_rows = pltpu.make_async_copy(
        rows_hbm.at[0, 0, :, pl.ds(pl.multiple_of(my_dp * share, LANES), share)], rows_all.at[my_dp], own_sem.at[0])
    own_rows.start()
    own_route = pltpu.make_async_copy(route_send.at[my_ep], route_recv.at[my_place], own_sem.at[1])
    own_route.start()
    own_route.wait()
    for copy in route_copies:
        copy.wait()

    diagonal = lax.broadcasted_iota(jnp.int32, (tokens, LANES), 0) == lax.broadcasted_iota(jnp.int32, (tokens, LANES), 1)
    for p in range(n_ep):
        spread = jnp.broadcast_to(route_recv[p], (tokens, LANES))
        route_col[p * tokens:(p + 1) * tokens, :] = jnp.broadcast_to(
            jnp.sum(jnp.where(diagonal, spread, 0.0), axis=1, keepdims=True), (tokens, LANES))
    chosen = jnp.where(route_col[...] > 0.0, 1.0, 0.0).astype(BF16)

    slot = lax.broadcasted_iota(jnp.int32, (slots, all_tokens), 0)
    token = lax.broadcasted_iota(jnp.int32, (slots, all_tokens), 1)
    same = slot // cap == reversed_bits(token // tokens, stages)
    counts = jnp.dot(jnp.where(same, 1.0, 0.0).astype(BF16), chosen, preferred_element_type=F32)
    within = lax.broadcasted_iota(jnp.int32, (slots, LANES), 0) % cap
    live = (within.astype(F32) < counts)[:, 0:1]

    for load in loads[:2]:
        load.wait()
    strip = LANES * 2
    for c in range(width // strip):
        cols = slice(c * strip, (c + 1) * strip)
        upper = slice(width + c * strip, width + (c + 1) * strip)
        g = gate_up[:, cols].astype(F32)
        u = gate_up[:, upper].astype(F32)
        h = hidden[:, cols].astype(F32)
        q = jax.nn.sigmoid(g)
        hq = h * q
        grads[:, cols] = jnp.where(live, hq * u * (1.0 + g * (1.0 - q)), 0.0).astype(BF16)
        grads[:, upper] = jnp.where(live, hq * g, 0.0).astype(BF16)
    grads_copies = []
    for k in range(1, n_dp):
        grads_copies.append(pltpu.make_async_remote_copy(
            src_ref=grads, dst_ref=grads_all.at[my_dp],
            send_sem=grads_ssem.at[k], recv_sem=grads_rsem.at[k],
            device_id={"dp": lax.rem(my_dp + k, n_dp)}, device_id_type=pl.DeviceIdType.MESH))
    for copy in grads_copies:
        copy.start()
    own_grads = pltpu.make_async_copy(grads, grads_all.at[my_dp], own_sem.at[2])
    own_grads.start()

    t0 = lax.broadcasted_iota(jnp.int32, (all_tokens, all_tokens), 0)
    t1 = lax.broadcasted_iota(jnp.int32, (all_tokens, all_tokens), 1)
    earlier = (t0 // tokens == t1 // tokens) & (t1 < t0)
    rank = jnp.dot(jnp.where(earlier, 1.0, 0.0).astype(BF16), chosen, preferred_element_type=F32)[:, 0:1]
    token_row = lax.broadcasted_iota(jnp.int32, (all_tokens, slots), 0)
    slot_col = lax.broadcasted_iota(jnp.int32, (all_tokens, slots), 1)
    offset = (slot_col - reversed_bits(token_row // tokens, stages) * cap).astype(F32)
    picks = jnp.where(offset == rank, 1.0, 0.0).astype(BF16)
    factor = route_col[:, 0:1]
    for c in range(width2 // strip):
        cols = slice(c * strip, (c + 1) * strip)
        moved = jnp.dot(picks, grads[:, cols], preferred_element_type=F32)
        mixed[:, cols] = (moved * factor).astype(BF16)

    loads[2].wait()
    half = all_tokens // 2
    step_cols = 256

    def product(which, part, put):
        left = mixed[pl.ds(pl.multiple_of(which * half, 16), half), :]
        for c in range(piece // step_cols):
            right = weight[part * piece + c * step_cols:part * piece + (c + 1) * step_cols, :]
            put(slice(c * step_cols, (c + 1) * step_cols),
                lax.dot_general(left, right, (((1,), (1,)), ((), ())), preferred_element_type=F32))

    def copy_of(stage, part):
        bit = (my_ep // 2**stage) % 2
        return pltpu.make_async_remote_copy(
            src_ref=sends[stage].at[part], dst_ref=recvs[stage].at[part],
            send_sem=half_ssem.at[stage, part], recv_sem=half_rsem.at[stage, part],
            device_id={"ep": my_ep + (1 - 2 * bit) * 2**stage}, device_id_type=pl.DeviceIdType.MESH)

    copies = {(s, part): copy_of(s, part) for s in range(stages) for part in range(PIECES)}
    first = my_ep % 2
    for part in range(PIECES):
        def put_send(cols, value, part=part):
            sends[0][part, :, cols] = value.astype(BF16)
        product(1 - first, part, put_send)
        copies[0, part].start()
    for part in range(PIECES):
        def put_keep(cols, value, part=part):
            total[part, :, cols] = value
        product(first, part, put_keep)

    base = my_ep * 0
    for s in range(1, stages + 1):
        if s < stages:
            size = all_tokens // 2**(s + 1)
            bit = (my_ep // 2**s) % 2
            give = pl.multiple_of((1 - bit) * size, 16)
            keep = pl.multiple_of(bit * size, 16)
            give_at = pl.multiple_of(base + (1 - bit) * size, 16)
            keep_at = pl.multiple_of(base + bit * size, 16)
            for part in range(PIECES):
                copies[s - 1, part].wait_recv()
                sends[s][part] = (total[part, pl.ds(give_at, size), :]
                                  + recvs[s - 1][part, pl.ds(give, size), :].astype(F32)).astype(BF16)
                copies[s, part].start()
                total[part, pl.ds(keep_at, size), :] = (
                    total[part, pl.ds(keep_at, size), :] + recvs[s - 1][part, pl.ds(keep, size), :].astype(F32))
            base = base + bit * size
        else:
            at = pl.multiple_of(base, 16)
            for part in range(PIECES):
                copies[s - 1, part].wait_recv()
                token_out[:, part * piece:(part + 1) * piece] = (
                    total[part, pl.ds(at, tokens), :] + recvs[s - 1][part].astype(F32)).astype(BF16)
    for copy in copies.values():
        copy.wait_send()
    own_rows.wait()
    own_grads.wait()
    for copy in rows_copies + grads_copies:
        copy.wait()


def weight_kernel(scale, rows_ref, grads_ref, token_ref, out_ref, token_out):
    @pl.when(pl.program_id(0) == 0)
    def _():
        token_out[...] = token_ref[...]

    n_dp, slots, block = rows_ref.shape
    width2 = grads_ref.shape[2]
    rows = rows_ref[...].reshape(n_dp * slots, block)
    strips = width2 // LANES
    chunk = 2 * LANES
    for c in range(width2 // chunk):
        grads = grads_ref[:, :, c * chunk:(c + 1) * chunk].reshape(n_dp * slots, chunk)
        value = lax.dot_general(rows, grads, (((0,), (0,)), ((), ())), preferred_element_type=F32) * scale
        for j in range(chunk // LANES):
            out_ref[pl.ds(c * (chunk // LANES) + j, block, stride=strips), :] = value[:, j * LANES:(j + 1) * LANES]


def shards(expert_ids, route_weights, saved_rows, saved_gate_up, hidden_grad, gate_up_weight):
    n_ep = lax.axis_size("ep")
    n_dp = lax.axis_size("dp")
    tokens, top = expert_ids.shape[1:]
    slots, model = saved_rows.shape[2:]
    width = hidden_grad.shape[3]
    width2 = 2 * width
    share = model // n_dp
    all_tokens = n_ep * tokens
    stages = n_ep.bit_length() - 1
    piece = model // PIECES
    vmem = pl.BlockSpec(memory_space=pltpu.VMEM)
    hbm = pl.BlockSpec(memory_space=pl.ANY)
    dma = pltpu.SemaphoreType.DMA
    parts = [pltpu.VMEM((PIECES, all_tokens // 2**(s + 1), piece), BF16) for s in range(stages)]
    rows_all, grads_all, token_grad = pl.pallas_call(
        functools.partial(exchange_kernel, n_dp, n_ep, stages),
        out_shape=(
            jax.ShapeDtypeStruct((n_dp, slots, share), BF16),
            jax.ShapeDtypeStruct((n_dp, slots, width2), BF16),
            jax.ShapeDtypeStruct((tokens, model), BF16),
        ),
        in_specs=[vmem, vmem, hbm, hbm, hbm, hbm],
        out_specs=(hbm, hbm, vmem),
        scratch_shapes=[
            pltpu.VMEM((n_ep, 1, LANES), F32),
            pltpu.VMEM((n_ep, 1, LANES), F32),
            pltpu.VMEM((all_tokens, LANES), F32),
            pltpu.VMEM((slots, width2), BF16),
            pltpu.VMEM((slots, width), BF16),
            pltpu.VMEM((model, width2), BF16),
            pltpu.VMEM((slots, width2), BF16),
            pltpu.VMEM((all_tokens, width2), BF16),
            pltpu.VMEM((PIECES, all_tokens // 2, piece), F32),
            dma((3,)), dma((3,)),
            dma((n_ep,)), dma((n_ep,)),
            dma((n_dp,)), dma((n_dp,)),
            dma((n_dp,)), dma((n_dp,)),
            dma((stages, PIECES)), dma((stages, PIECES)),
            *parts, *parts,
        ],
        compiler_params=pltpu.CompilerParams(
            collective_id=0, has_side_effects=True, vmem_limit_bytes=VMEM_LIMIT),
    )(
        expert_ids.reshape(tokens, top).T, route_weights.reshape(tokens, top).T,
        saved_rows, saved_gate_up, hidden_grad, gate_up_weight,
    )
    block = min(share, 128)
    strips = width2 // LANES
    flat, token_grad = pl.pallas_call(
        functools.partial(weight_kernel, 1.0 / n_dp),
        grid=(share // block,),
        out_shape=(
            jax.ShapeDtypeStruct((share * strips, LANES), F32),
            jax.ShapeDtypeStruct((tokens, model), BF16),
        ),
        in_specs=[
            pl.BlockSpec((n_dp, slots, block), lambda i: (0, 0, i)),
            pl.BlockSpec((n_dp, slots, width2), lambda i: (0, 0, 0)),
            pl.BlockSpec((tokens, model), lambda i: (0, 0)),
        ],
        out_specs=(
            pl.BlockSpec((block * strips, LANES), lambda i: (i, 0)),
            pl.BlockSpec((tokens, model), lambda i: (0, 0)),
        ),
        compiler_params=pltpu.CompilerParams(vmem_limit_bytes=VMEM_LIMIT),
    )(rows_all, grads_all, token_grad)
    return token_grad.reshape(1, tokens, model), flat.reshape(share, 1, width2)


def solution(mesh):
    in_specs = (
        P("dp", "ep", None),
        P("dp", "ep", None),
        P("dp", "ep", None, None),
        P("dp", "ep", None, None),
        P("dp", "ep", None, None),
        P("ep", None, None),
    )
    out_specs = (P("dp", "ep", None), P("dp", "ep", None))
    return jax.shard_map(shards, mesh=mesh, in_specs=in_specs, out_specs=out_specs, check_vma=False)
```

```python
import functools

import jax
import jax.numpy as jnp
from jax import lax
from jax.experimental import pallas as pl
from jax.experimental.pallas import tpu as pltpu
from jax.sharding import PartitionSpec as P

F32 = jnp.float32
BF16 = jnp.bfloat16
LANES = 128
PIECES = 2
VMEM_LIMIT = 56 * 2**20


def reversed_bits(value, bits):
    out = value * 0
    for b in range(bits):
        out = out * 2 + (value // 2**b) % 2
    return out


def exchange_kernel(
    n_dp, n_ep, stages, ids_ref, route_ref, rows_hbm, gate_up_hbm, hidden_hbm, weight_hbm,
    rows_all, grads_all, token_out,
    route_rows, route_col, gate_up, hidden, weight, grads, mixed, total,
    load_sem, own_sem, route_ssem, route_rsem, rows_ssem, rows_rsem, grads_ssem, grads_rsem,
    half_ssem, half_rsem, *halves,
):
    sends, recvs, route_sends, route_recvs = (halves[i * stages:(i + 1) * stages] for i in range(4))
    my_dp = lax.axis_index("dp")
    my_ep = lax.axis_index("ep")
    tokens = ids_ref.shape[1]
    slots, width2 = grads.shape
    width = width2 // 2
    model = weight.shape[0]
    share = model // n_dp
    cap = slots // n_ep
    all_tokens = n_ep * tokens
    piece = model // PIECES

    loads = [
        pltpu.make_async_copy(gate_up_hbm.at[0, 0], gate_up, load_sem.at[0]),
        pltpu.make_async_copy(hidden_hbm.at[0, 0], hidden, load_sem.at[1]),
        pltpu.make_async_copy(weight_hbm.at[0], weight, load_sem.at[2]),
    ]
    for load in loads:
        load.start()

    bits = [(my_ep // 2**stage) % 2 for stage in range(stages)]
    partners = [my_ep + (1 - 2 * bits[stage]) * 2**stage for stage in range(stages)]
    barrier = pltpu.get_barrier_semaphore()
    for k in range(1, n_dp):
        pl.semaphore_signal(barrier, inc=1, device_id={"dp": lax.rem(my_dp + k, n_dp)}, device_id_type=pl.DeviceIdType.MESH)
    for partner in partners:
        pl.semaphore_signal(barrier, inc=1, device_id={"ep": partner}, device_id_type=pl.DeviceIdType.MESH)

    route_rows[...] = jnp.zeros_like(route_rows)
    ids = ids_ref[...]
    route = route_ref[...]
    for x in range(n_ep):
        route_rows[x, :, 0:tokens] = jnp.sum(jnp.where(ids == x, route, 0.0), axis=0, keepdims=True)
    pl.semaphore_wait(barrier, n_dp - 1 + stages)

    rows_copies = []
    for k in range(1, n_dp):
        to = lax.rem(my_dp + k, n_dp)
        rows_copies.append(pltpu.make_async_remote_copy(
            src_ref=rows_hbm.at[0, 0, :, pl.ds(pl.multiple_of(to * share, LANES), share)],
            dst_ref=rows_all.at[my_dp],
            send_sem=rows_ssem.at[k], recv_sem=rows_rsem.at[k],
            device_id={"dp": to}, device_id_type=pl.DeviceIdType.MESH))
    for copy in rows_copies:
        copy.start()

    route_copies = []

    def entry(stage, i):
        return i // 2**stage * 2**(stage + 1) + (1 - bits[stage]) * 2**stage + i % 2**stage

    def route_start(stage):
        for i in range(n_ep // 2):
            route_sends[stage][i] = route_rows[entry(stage, i)]
        copy = pltpu.make_async_remote_copy(
            src_ref=route_sends[stage], dst_ref=route_recvs[stage],
            send_sem=route_ssem.at[stage], recv_sem=route_rsem.at[stage],
            device_id={"ep": partners[stage]}, device_id_type=pl.DeviceIdType.MESH)
        copy.start()
        route_copies.append(copy)

    def route_finish(stage):
        route_copies[stage].wait()
        for i in range(n_ep // 2):
            route_rows[entry(stage, i)] = route_recvs[stage][i]

    route_start(0)
    own_rows = pltpu.make_async_copy(
        rows_hbm.at[0, 0, :, pl.ds(pl.multiple_of(my_dp * share, LANES), share)], rows_all.at[my_dp], own_sem.at[0])
    own_rows.start()
    for load in loads[:2]:
        load.wait()
    strip = LANES * 2
    strips = width // strip

    def slot_strips(first, last):
        for c in range(first, last):
            cols = slice(c * strip, (c + 1) * strip)
            upper = slice(width + c * strip, width + (c + 1) * strip)
            g = gate_up[:, cols].astype(F32)
            u = gate_up[:, upper].astype(F32)
            h = hidden[:, cols].astype(F32)
            q = jax.nn.sigmoid(g)
            hq = h * q
            grads[:, cols] = (hq * u * (1.0 + g * (1.0 - q))).astype(BF16)
            grads[:, upper] = (hq * g).astype(BF16)

    for stage in range(stages):
        slot_strips(strips * stage // stages, strips * (stage + 1) // stages)
        route_finish(stage)
        if stage + 1 < stages:
            route_start(stage + 1)

    diagonal = lax.broadcasted_iota(jnp.int32, (tokens, LANES), 0) == lax.broadcasted_iota(jnp.int32, (tokens, LANES), 1)
    for p in range(n_ep):
        spread = jnp.broadcast_to(route_rows[reversed_bits(p, stages)], (tokens, LANES))
        route_col[p * tokens:(p + 1) * tokens, :] = jnp.broadcast_to(
            jnp.sum(jnp.where(diagonal, spread, 0.0), axis=1, keepdims=True), (tokens, LANES))
    chosen = jnp.where(route_col[...] > 0.0, 1.0, 0.0).astype(BF16)

    slot = lax.broadcasted_iota(jnp.int32, (slots, all_tokens), 0)
    token = lax.broadcasted_iota(jnp.int32, (slots, all_tokens), 1)
    same = slot // cap == reversed_bits(token // tokens, stages)
    counts = jnp.dot(jnp.where(same, 1.0, 0.0).astype(BF16), chosen, preferred_element_type=F32)
    within = lax.broadcasted_iota(jnp.int32, (slots, LANES), 0) % cap
    live = (within.astype(F32) < counts)[:, 0:1]

    for c in range(width2 // strip):
        cols = slice(c * strip, (c + 1) * strip)
        grads[:, cols] = jnp.where(live, grads[:, cols].astype(F32), 0.0).astype(BF16)
    grads_copies = []
    for k in range(1, n_dp):
        grads_copies.append(pltpu.make_async_remote_copy(
            src_ref=grads, dst_ref=grads_all.at[my_dp],
            send_sem=grads_ssem.at[k], recv_sem=grads_rsem.at[k],
            device_id={"dp": lax.rem(my_dp + k, n_dp)}, device_id_type=pl.DeviceIdType.MESH))
    for copy in grads_copies:
        copy.start()
    own_grads = pltpu.make_async_copy(grads, grads_all.at[my_dp], own_sem.at[2])
    own_grads.start()

    t0 = lax.broadcasted_iota(jnp.int32, (all_tokens, all_tokens), 0)
    t1 = lax.broadcasted_iota(jnp.int32, (all_tokens, all_tokens), 1)
    earlier = (t0 // tokens == t1 // tokens) & (t1 < t0)
    rank = jnp.dot(jnp.where(earlier, 1.0, 0.0).astype(BF16), chosen, preferred_element_type=F32)[:, 0:1]
    token_row = lax.broadcasted_iota(jnp.int32, (all_tokens, slots), 0)
    slot_col = lax.broadcasted_iota(jnp.int32, (all_tokens, slots), 1)
    offset = (slot_col - reversed_bits(token_row // tokens, stages) * cap).astype(F32)
    picks = jnp.where(offset == rank, 1.0, 0.0).astype(BF16)
    factor = route_col[:, 0:1]
    for c in range(width2 // strip):
        cols = slice(c * strip, (c + 1) * strip)
        moved = jnp.dot(picks, grads[:, cols], preferred_element_type=F32)
        mixed[:, cols] = (moved * factor).astype(BF16)

    loads[2].wait()
    half = all_tokens // 2
    step_cols = 256

    def product(which, part, put):
        left = mixed[pl.ds(pl.multiple_of(which * half, 16), half), :]
        for c in range(piece // step_cols):
            right = weight[part * piece + c * step_cols:part * piece + (c + 1) * step_cols, :]
            put(slice(c * step_cols, (c + 1) * step_cols),
                lax.dot_general(left, right, (((1,), (1,)), ((), ())), preferred_element_type=F32))

    def copy_of(stage, part):
        return pltpu.make_async_remote_copy(
            src_ref=sends[stage].at[part], dst_ref=recvs[stage].at[part],
            send_sem=half_ssem.at[stage, part], recv_sem=half_rsem.at[stage, part],
            device_id={"ep": partners[stage]}, device_id_type=pl.DeviceIdType.MESH)

    copies = {(s, part): copy_of(s, part) for s in range(stages) for part in range(PIECES)}
    first = my_ep % 2
    for part in range(PIECES):
        def put_send(cols, value, part=part):
            sends[0][part, :, cols] = value.astype(BF16)
        product(1 - first, part, put_send)
        copies[0, part].start()
    for part in range(PIECES):
        def put_keep(cols, value, part=part):
            total[part, :, cols] = value
        product(first, part, put_keep)

    base = my_ep * 0
    for s in range(1, stages + 1):
        if s < stages:
            size = all_tokens // 2**(s + 1)
            bit = bits[s]
            give = pl.multiple_of((1 - bit) * size, 16)
            keep = pl.multiple_of(bit * size, 16)
            give_at = pl.multiple_of(base + (1 - bit) * size, 16)
            keep_at = pl.multiple_of(base + bit * size, 16)
            for part in range(PIECES):
                copies[s - 1, part].wait_recv()
                sends[s][part] = (total[part, pl.ds(give_at, size), :]
                                  + recvs[s - 1][part, pl.ds(give, size), :].astype(F32)).astype(BF16)
                copies[s, part].start()
                total[part, pl.ds(keep_at, size), :] = (
                    total[part, pl.ds(keep_at, size), :] + recvs[s - 1][part, pl.ds(keep, size), :].astype(F32))
            base = base + bit * size
        else:
            at = pl.multiple_of(base, 16)
            for part in range(PIECES):
                copies[s - 1, part].wait_recv()
                token_out[:, part * piece:(part + 1) * piece] = (
                    total[part, pl.ds(at, tokens), :] + recvs[s - 1][part].astype(F32)).astype(BF16)
    for copy in copies.values():
        copy.wait_send()
    own_rows.wait()
    own_grads.wait()
    for copy in rows_copies + grads_copies:
        copy.wait()


def weight_kernel(scale, rows_ref, grads_ref, token_ref, out_ref, token_out):
    @pl.when(pl.program_id(0) == 0)
    def _():
        token_out[...] = token_ref[...]

    n_dp, slots, block = rows_ref.shape
    width2 = grads_ref.shape[2]
    rows = rows_ref[...].reshape(n_dp * slots, block)
    strips = width2 // LANES
    chunk = 2 * LANES
    for c in range(width2 // chunk):
        grads = grads_ref[:, :, c * chunk:(c + 1) * chunk].reshape(n_dp * slots, chunk)
        value = lax.dot_general(rows, grads, (((0,), (0,)), ((), ())), preferred_element_type=F32) * scale
        for j in range(chunk // LANES):
            out_ref[pl.ds(c * (chunk // LANES) + j, block, stride=strips), :] = value[:, j * LANES:(j + 1) * LANES]


def shards(expert_ids, route_weights, saved_rows, saved_gate_up, hidden_grad, gate_up_weight):
    n_ep = lax.axis_size("ep")
    n_dp = lax.axis_size("dp")
    tokens, top = expert_ids.shape[1:]
    slots, model = saved_rows.shape[2:]
    width = hidden_grad.shape[3]
    width2 = 2 * width
    share = model // n_dp
    all_tokens = n_ep * tokens
    stages = n_ep.bit_length() - 1
    piece = model // PIECES
    vmem = pl.BlockSpec(memory_space=pltpu.VMEM)
    hbm = pl.BlockSpec(memory_space=pl.ANY)
    dma = pltpu.SemaphoreType.DMA
    parts = [pltpu.VMEM((PIECES, all_tokens // 2**(s + 1), piece), BF16) for s in range(stages)]
    routes = [pltpu.VMEM((n_ep // 2, 1, LANES), F32)] * stages
    rows_all, grads_all, token_grad = pl.pallas_call(
        functools.partial(exchange_kernel, n_dp, n_ep, stages),
        out_shape=(
            jax.ShapeDtypeStruct((n_dp, slots, share), BF16),
            jax.ShapeDtypeStruct((n_dp, slots, width2), BF16),
            jax.ShapeDtypeStruct((tokens, model), BF16),
        ),
        in_specs=[vmem, vmem, hbm, hbm, hbm, hbm],
        out_specs=(hbm, hbm, vmem),
        scratch_shapes=[
            pltpu.VMEM((n_ep, 1, LANES), F32),
            pltpu.VMEM((all_tokens, LANES), F32),
            pltpu.VMEM((slots, width2), BF16),
            pltpu.VMEM((slots, width), BF16),
            pltpu.VMEM((model, width2), BF16),
            pltpu.VMEM((slots, width2), BF16),
            pltpu.VMEM((all_tokens, width2), BF16),
            pltpu.VMEM((PIECES, all_tokens // 2, piece), F32),
            dma((3,)), dma((3,)),
            dma((stages,)), dma((stages,)),
            dma((n_dp,)), dma((n_dp,)),
            dma((n_dp,)), dma((n_dp,)),
            dma((stages, PIECES)), dma((stages, PIECES)),
            *parts, *parts, *routes, *routes,
        ],
        compiler_params=pltpu.CompilerParams(
            collective_id=0, has_side_effects=True, vmem_limit_bytes=VMEM_LIMIT),
    )(
        expert_ids.reshape(tokens, top).T, route_weights.reshape(tokens, top).T,
        saved_rows, saved_gate_up, hidden_grad, gate_up_weight,
    )
    block = min(share, 512)
    strips = width2 // LANES
    flat, token_grad = pl.pallas_call(
        functools.partial(weight_kernel, 1.0 / n_dp),
        grid=(share // block,),
        out_shape=(
            jax.ShapeDtypeStruct((share * strips, LANES), F32),
            jax.ShapeDtypeStruct((tokens, model), BF16),
        ),
        in_specs=[
            pl.BlockSpec((n_dp, slots, block), lambda i: (0, 0, i)),
            pl.BlockSpec((n_dp, slots, width2), lambda i: (0, 0, 0)),
            pl.BlockSpec((tokens, model), lambda i: (0, 0)),
        ],
        out_specs=(
            pl.BlockSpec((block * strips, LANES), lambda i: (i, 0)),
            pl.BlockSpec((tokens, model), lambda i: (0, 0)),
        ),
        compiler_params=pltpu.CompilerParams(vmem_limit_bytes=VMEM_LIMIT),
    )(rows_all, grads_all, token_grad)
    return token_grad.reshape(1, tokens, model), flat.reshape(share, 1, width2)


def solution(mesh):
    in_specs = (
        P("dp", "ep", None),
        P("dp", "ep", None),
        P("dp", "ep", None, None),
        P("dp", "ep", None, None),
        P("dp", "ep", None, None),
        P("ep", None, None),
    )
    out_specs = (P("dp", "ep", None), P("dp", "ep", None))
    return jax.shard_map(shards, mesh=mesh, in_specs=in_specs, out_specs=out_specs, check_vma=False)
```

```python
import functools

import jax
import jax.numpy as jnp
from jax import lax
from jax.experimental import pallas as pl
from jax.experimental.pallas import tpu as pltpu
from jax.sharding import PartitionSpec as P

F32 = jnp.float32
BF16 = jnp.bfloat16
LANES = 128
PIECES = 2
VMEM_LIMIT = 40 * 2**20


def reversed_bits(value, bits):
    out = value * 0
    for b in range(bits):
        out = out * 2 + (value // 2**b) % 2
    return out


def exchange_kernel(
    n_dp, n_ep, stages, ids_ref, route_ref, rows_hbm, gate_up_hbm, hidden_hbm, weight_hbm,
    rows_all, grads_all, token_out,
    route_rows, route_col, gate_up, hidden, weight, grads, mixed, total,
    load_sem, own_sem, route_ssem, route_rsem, rows_ssem, rows_rsem, grads_ssem, grads_rsem,
    half_ssem, half_rsem, *halves,
):
    sends, recvs, route_sends, route_recvs = (halves[i * stages:(i + 1) * stages] for i in range(4))
    my_dp = lax.axis_index("dp")
    my_ep = lax.axis_index("ep")
    tokens = ids_ref.shape[1]
    slots, width2 = grads.shape
    width = width2 // 2
    model = weight.shape[0]
    share = model // n_dp
    cap = slots // n_ep
    all_tokens = n_ep * tokens
    piece = model // PIECES

    loads = [
        pltpu.make_async_copy(gate_up_hbm.at[0, 0], gate_up, load_sem.at[0]),
        pltpu.make_async_copy(hidden_hbm.at[0, 0], hidden, load_sem.at[1]),
        pltpu.make_async_copy(weight_hbm.at[0], weight, load_sem.at[2]),
    ]
    for load in loads:
        load.start()

    bits = [(my_ep // 2**stage) % 2 for stage in range(stages)]
    partners = [my_ep + (1 - 2 * bits[stage]) * 2**stage for stage in range(stages)]
    barrier = pltpu.get_barrier_semaphore()
    for k in range(1, n_dp):
        pl.semaphore_signal(barrier, inc=1, device_id={"dp": lax.rem(my_dp + k, n_dp)}, device_id_type=pl.DeviceIdType.MESH)
    for partner in partners:
        pl.semaphore_signal(barrier, inc=1, device_id={"ep": partner}, device_id_type=pl.DeviceIdType.MESH)

    route_rows[...] = jnp.zeros_like(route_rows)
    ids = ids_ref[...]
    route = route_ref[...]
    for x in range(n_ep):
        route_rows[x, :, 0:tokens] = jnp.sum(jnp.where(ids == x, route, 0.0), axis=0, keepdims=True)
    pl.semaphore_wait(barrier, n_dp - 1 + stages)

    rows_copies = []
    for k in range(1, n_dp):
        to = lax.rem(my_dp + k, n_dp)
        rows_copies.append(pltpu.make_async_remote_copy(
            src_ref=rows_hbm.at[0, 0, :, pl.ds(pl.multiple_of(to * share, LANES), share)],
            dst_ref=rows_all.at[my_dp],
            send_sem=rows_ssem.at[k], recv_sem=rows_rsem.at[k],
            device_id={"dp": to}, device_id_type=pl.DeviceIdType.MESH))
    for copy in rows_copies:
        copy.start()

    route_copies = []

    def entry(stage, i):
        return i // 2**stage * 2**(stage + 1) + (1 - bits[stage]) * 2**stage + i % 2**stage

    def route_start(stage):
        for i in range(n_ep // 2):
            route_sends[stage][i] = route_rows[entry(stage, i)]
        copy = pltpu.make_async_remote_copy(
            src_ref=route_sends[stage], dst_ref=route_recvs[stage],
            send_sem=route_ssem.at[stage], recv_sem=route_rsem.at[stage],
            device_id={"ep": partners[stage]}, device_id_type=pl.DeviceIdType.MESH)
        copy.start()
        route_copies.append(copy)

    def route_finish(stage):
        route_copies[stage].wait()
        for i in range(n_ep // 2):
            route_rows[entry(stage, i)] = route_recvs[stage][i]

    route_start(0)
    own_rows = pltpu.make_async_copy(
        rows_hbm.at[0, 0, :, pl.ds(pl.multiple_of(my_dp * share, LANES), share)], rows_all.at[my_dp], own_sem.at[0])
    own_rows.start()
    for load in loads[:2]:
        load.wait()
    strip = LANES * 2
    strips = width // strip

    def slot_strips(first, last):
        for c in range(first, last):
            cols = slice(c * strip, (c + 1) * strip)
            upper = slice(width + c * strip, width + (c + 1) * strip)
            g = gate_up[:, cols].astype(F32)
            u = gate_up[:, upper].astype(F32)
            h = hidden[:, cols].astype(F32)
            q = jax.nn.sigmoid(g)
            hq = h * q
            grads[:, cols] = (hq * u * (1.0 + g * (1.0 - q))).astype(BF16)
            grads[:, upper] = (hq * g).astype(BF16)

    for stage in range(stages):
        slot_strips(strips * stage // stages, strips * (stage + 1) // stages)
        route_finish(stage)
        if stage + 1 < stages:
            route_start(stage + 1)

    diagonal = lax.broadcasted_iota(jnp.int32, (tokens, LANES), 0) == lax.broadcasted_iota(jnp.int32, (tokens, LANES), 1)
    for p in range(n_ep):
        spread = jnp.broadcast_to(route_rows[reversed_bits(p, stages)], (tokens, LANES))
        route_col[p * tokens:(p + 1) * tokens, :] = jnp.broadcast_to(
            jnp.sum(jnp.where(diagonal, spread, 0.0), axis=1, keepdims=True), (tokens, LANES))
    chosen = jnp.where(route_col[...] > 0.0, 1.0, 0.0).astype(BF16)

    slot = lax.broadcasted_iota(jnp.int32, (slots, all_tokens), 0)
    token = lax.broadcasted_iota(jnp.int32, (slots, all_tokens), 1)
    same = slot // cap == reversed_bits(token // tokens, stages)
    counts = jnp.dot(jnp.where(same, 1.0, 0.0).astype(BF16), chosen, preferred_element_type=F32)
    within = lax.broadcasted_iota(jnp.int32, (slots, LANES), 0) % cap
    live = (within.astype(F32) < counts)[:, 0:1]

    for c in range(width2 // strip):
        cols = slice(c * strip, (c + 1) * strip)
        grads[:, cols] = jnp.where(live, grads[:, cols].astype(F32), 0.0).astype(BF16)
    grads_copies = []
    for k in range(1, n_dp):
        grads_copies.append(pltpu.make_async_remote_copy(
            src_ref=grads, dst_ref=grads_all.at[my_dp],
            send_sem=grads_ssem.at[k], recv_sem=grads_rsem.at[k],
            device_id={"dp": lax.rem(my_dp + k, n_dp)}, device_id_type=pl.DeviceIdType.MESH))
    for copy in grads_copies:
        copy.start()
    own_grads = pltpu.make_async_copy(grads, grads_all.at[my_dp], own_sem.at[2])
    own_grads.start()

    t0 = lax.broadcasted_iota(jnp.int32, (all_tokens, all_tokens), 0)
    t1 = lax.broadcasted_iota(jnp.int32, (all_tokens, all_tokens), 1)
    earlier = (t0 // tokens == t1 // tokens) & (t1 < t0)
    rank = jnp.dot(jnp.where(earlier, 1.0, 0.0).astype(BF16), chosen, preferred_element_type=F32)[:, 0:1]
    token_row = lax.broadcasted_iota(jnp.int32, (all_tokens, slots), 0)
    slot_col = lax.broadcasted_iota(jnp.int32, (all_tokens, slots), 1)
    offset = (slot_col - reversed_bits(token_row // tokens, stages) * cap).astype(F32)
    picks = jnp.where(offset == rank, 1.0, 0.0).astype(BF16)
    factor = route_col[:, 0:1]
    for c in range(width2 // strip):
        cols = slice(c * strip, (c + 1) * strip)
        moved = jnp.dot(picks, grads[:, cols], preferred_element_type=F32)
        mixed[:, cols] = (moved * factor).astype(BF16)

    loads[2].wait()
    half = all_tokens // 2
    step_cols = 256

    def product(which, part, put):
        left = mixed[pl.ds(pl.multiple_of(which * half, 16), half), :]
        for c in range(piece // step_cols):
            right = weight[part * piece + c * step_cols:part * piece + (c + 1) * step_cols, :]
            put(slice(c * step_cols, (c + 1) * step_cols),
                lax.dot_general(left, right, (((1,), (1,)), ((), ())), preferred_element_type=F32))

    def copy_of(stage, part):
        return pltpu.make_async_remote_copy(
            src_ref=sends[stage].at[part], dst_ref=recvs[stage].at[part],
            send_sem=half_ssem.at[stage, part], recv_sem=half_rsem.at[stage, part],
            device_id={"ep": partners[stage]}, device_id_type=pl.DeviceIdType.MESH)

    copies = {(s, part): copy_of(s, part) for s in range(stages) for part in range(PIECES)}
    first = my_ep % 2
    for part in range(PIECES):
        def put_send(cols, value, part=part):
            sends[0][part, :, cols] = value.astype(BF16)
        product(1 - first, part, put_send)
        copies[0, part].start()
    for part in range(PIECES):
        def put_keep(cols, value, part=part):
            total[part, :, cols] = value
        product(first, part, put_keep)

    base = my_ep * 0
    for s in range(1, stages + 1):
        if s < stages:
            size = all_tokens // 2**(s + 1)
            bit = bits[s]
            give = pl.multiple_of((1 - bit) * size, 16)
            keep = pl.multiple_of(bit * size, 16)
            give_at = pl.multiple_of(base + (1 - bit) * size, 16)
            keep_at = pl.multiple_of(base + bit * size, 16)
            for part in range(PIECES):
                copies[s - 1, part].wait_recv()
                sends[s][part] = (total[part, pl.ds(give_at, size), :]
                                  + recvs[s - 1][part, pl.ds(give, size), :].astype(F32)).astype(BF16)
                copies[s, part].start()
                total[part, pl.ds(keep_at, size), :] = (
                    total[part, pl.ds(keep_at, size), :] + recvs[s - 1][part, pl.ds(keep, size), :].astype(F32))
            base = base + bit * size
        else:
            at = pl.multiple_of(base, 16)
            for part in range(PIECES):
                copies[s - 1, part].wait_recv()
                token_out[:, part * piece:(part + 1) * piece] = (
                    total[part, pl.ds(at, tokens), :] + recvs[s - 1][part].astype(F32)).astype(BF16)
    for copy in copies.values():
        copy.wait_send()
    own_rows.wait()
    own_grads.wait()
    for copy in rows_copies + grads_copies:
        copy.wait()


def weight_kernel(scale, rows, grads, token_ref, out_hbm, token_out, out, out_sem):
    n_dp, slots, share = rows.shape
    width2 = grads.shape[2]
    depth = n_dp * slots
    strips = width2 // LANES
    chunk = 2 * LANES
    part = width2 // 1
    block = min(share, 128)
    token_out[...] = token_ref[...]
    stores = []
    for m in range(share // block):
        left = rows[:, :, m * block:(m + 1) * block].reshape(depth, block)
        for c in range(width2 // chunk):
            right = grads[:, :, c * chunk:(c + 1) * chunk].reshape(depth, chunk)
            value = lax.dot_general(left, right, (((0,), (0,)), ((), ())), preferred_element_type=F32) * scale
            for j in range(chunk // LANES):
                at = m * block * strips + c * (chunk // LANES) + j
                out[pl.ds(at, block, stride=strips), :] = value[:, j * LANES:(j + 1) * LANES]
        band = pl.ds(m * block * strips, block * strips)
        stores.append(pltpu.make_async_copy(out.at[band], out_hbm.at[band], out_sem.at[m]))
        stores[m].start()
    for store in stores:
        store.wait()


def shards(expert_ids, route_weights, saved_rows, saved_gate_up, hidden_grad, gate_up_weight):
    n_ep = lax.axis_size("ep")
    n_dp = lax.axis_size("dp")
    tokens, top = expert_ids.shape[1:]
    slots, model = saved_rows.shape[2:]
    width = hidden_grad.shape[3]
    width2 = 2 * width
    share = model // n_dp
    all_tokens = n_ep * tokens
    stages = n_ep.bit_length() - 1
    piece = model // PIECES
    vmem = pl.BlockSpec(memory_space=pltpu.VMEM)
    hbm = pl.BlockSpec(memory_space=pl.ANY)
    dma = pltpu.SemaphoreType.DMA
    parts = [pltpu.VMEM((PIECES, all_tokens // 2**(s + 1), piece), BF16) for s in range(stages)]
    routes = [pltpu.VMEM((n_ep // 2, 1, LANES), F32)] * stages
    rows_all, grads_all, token_grad = pl.pallas_call(
        functools.partial(exchange_kernel, n_dp, n_ep, stages),
        out_shape=(
            pltpu.VMEM((n_dp, slots, share), BF16),
            pltpu.VMEM((n_dp, slots, width2), BF16),
            jax.ShapeDtypeStruct((tokens, model), BF16),
        ),
        in_specs=[vmem, vmem, hbm, hbm, hbm, hbm],
        out_specs=(vmem, vmem, vmem),
        scratch_shapes=[
            pltpu.VMEM((n_ep, 1, LANES), F32),
            pltpu.VMEM((all_tokens, LANES), F32),
            pltpu.VMEM((slots, width2), BF16),
            pltpu.VMEM((slots, width), BF16),
            pltpu.VMEM((model, width2), BF16),
            pltpu.VMEM((slots, width2), BF16),
            pltpu.VMEM((all_tokens, width2), BF16),
            pltpu.VMEM((PIECES, all_tokens // 2, piece), F32),
            dma((3,)), dma((3,)),
            dma((stages,)), dma((stages,)),
            dma((n_dp,)), dma((n_dp,)),
            dma((n_dp,)), dma((n_dp,)),
            dma((stages, PIECES)), dma((stages, PIECES)),
            *parts, *parts, *routes, *routes,
        ],
        compiler_params=pltpu.CompilerParams(
            collective_id=0, has_side_effects=True, vmem_limit_bytes=VMEM_LIMIT),
    )(
        expert_ids.reshape(tokens, top).T, route_weights.reshape(tokens, top).T,
        *(pltpu.with_memory_space_constraint(x, pltpu.HBM) for x in (saved_rows, saved_gate_up, hidden_grad, gate_up_weight)),
    )
    strips = width2 // LANES
    flat, token_grad = pl.pallas_call(
        functools.partial(weight_kernel, 1.0 / n_dp),
        out_shape=(
            jax.ShapeDtypeStruct((share * strips, LANES), F32),
            jax.ShapeDtypeStruct((tokens, model), BF16),
        ),
        in_specs=[vmem, vmem, vmem],
        out_specs=(hbm, vmem),
        scratch_shapes=[
            pltpu.VMEM((share * strips, LANES), F32),
            dma((share // min(share, 128),)),
        ],
        compiler_params=pltpu.CompilerParams(vmem_limit_bytes=VMEM_LIMIT),
    )(rows_all, grads_all, token_grad)
    return token_grad.reshape(1, tokens, model), flat.reshape(share, 1, width2)


def solution(mesh):
    in_specs = (
        P("dp", "ep", None),
        P("dp", "ep", None),
        P("dp", "ep", None, None),
        P("dp", "ep", None, None),
        P("dp", "ep", None, None),
        P("ep", None, None),
    )
    out_specs = (P("dp", "ep", None), P("dp", "ep", None))
    return jax.shard_map(shards, mesh=mesh, in_specs=in_specs, out_specs=out_specs, check_vma=False)
```
